128 devices in a mesh: tm: 16 (over x, y), rows: 8 (over z, core).
Axes of the slice: x: 4, y: 4, z: 4, core: 2. Of those that a mesh axis runs over, the one named last changes fastest.
Arguments:
- latents: bfloat16 [32, 64, 64, 384], P('tm', 'rows'), may hold values from -6 to 6
- gain_one: float32 [384], replicated, may hold values from 0.1 to 1.9
- conv_one: bfloat16 [3, 3, 3, 384, 384], replicated, may hold values from -0.0625 to 0.0625
- up_weight: bfloat16 [384, 384], replicated, may hold values from -0.3125 to 0.3125
- gain_two: float32 [192], replicated, may hold values from 0.1 to 1.9
- conv_two: bfloat16 [3, 3, 3, 192, 192], replicated, may hold values from -0.078125 to 0.078125
- frame_counts: int32 [16], replicated, may hold values from 1 to 4, as said below
- row_counts: int32 [8], replicated, may hold values from 4 to 8, as said below
Outputs:
- decoded: bfloat16 [64, 64, 64, 192], P('tm', 'rows')
The draws below stay inside these ranges and needn't reach their ends.
Inputs may be any that keep to these rules, and one draw needn't show every extreme that they name: The live slots of time shard i are its first frame_counts[i] slots; some shard has 4 live slots and some has one. The frame rows of strip j are its first row_counts[j] row slots; some strip holds 8 rows and some holds 4.
All inputs are finite; a program needn't handle non-finite values.
Results may differ from the reference program's by a relative error of at most 0.0062.
Values may be sent and summed in bfloat16 or wider, within the bound.
A program may use at most 128 MiB of HBM per device.

```python
import jax
import jax.numpy as jnp
from jax import lax

C1 = 384
C2 = 192
HS = 8
W = 64
FUP = 4
LATENT_FRAMES = 32
HEIGHT = 64
SLOTS = 64
N_TM = 16
N_ROWS = 8


def draw_frame_counts(key, part):
    key = jax.random.fold_in(key, 11)
    first_key, second_key = jax.random.split(key)
    values = jax.random.randint(first_key, (N_TM,), 1, FUP + 1, dtype=jnp.int32)
    places = jax.random.permutation(second_key, N_TM)
    values = values.at[places[0]].set(FUP)
    values = values.at[places[1]].set(1)
    return values.astype(jnp.int32)


def draw_row_counts(key, part):
    key = jax.random.fold_in(key, 23)
    first_key, second_key = jax.random.split(key)
    values = jax.random.randint(first_key, (N_ROWS,), HS // 2, HS + 1, dtype=jnp.int32)
    places = jax.random.permutation(second_key, N_ROWS)
    values = values.at[places[0]].set(HS)
    values = values.at[places[1]].set(HS // 2)
    return values.astype(jnp.int32)


def steps_of(own_key, extent, cuts, low, largest):
    level, own = 1.0, jax.random.fold_in(own_key, 6)
    for dim, shards_of in cuts:
        heights = jnp.exp(jax.random.uniform(jax.random.fold_in(own, dim), (shards_of,), jnp.float32, low / len(cuts), largest / len(cuts)))
        level = level * jnp.repeat(heights, extent[dim] // shards_of).reshape([-1 if axis == dim else 1 for axis in range(len(extent))])
    return level


def centred(rng, dims, scale, bound, shards=(), kind=jnp.bfloat16):
    drawn = scale * jax.random.normal(rng, dims, jnp.float32)
    if shards:
        drawn = drawn * steps_of(rng, dims, shards, -0.22, 0.18)
    return jnp.clip(drawn, -bound, bound).astype(kind)


def setup_inputs(seed: int = 0) -> dict:
    arg_keys = jax.random.split(jax.random.key(seed), 9)
    return {
        "latents": centred(arg_keys[0], (LATENT_FRAMES, HEIGHT, W, C1), 1.0, 6.0, ((0, 16), (1, 8))),
        "gain_one": jnp.clip(1.0 + 0.18 * jax.random.normal(arg_keys[1], (C1,), jnp.float32), 0.1, 1.9),
        "conv_one": centred(arg_keys[2], (3, 3, 3, C1, C1), (27 * C1) ** -0.5, 0.0625),
        "up_weight": centred(arg_keys[3], (C1, 2 * C2), C1 ** -0.5, 0.3125),
        "gain_two": jnp.clip(1.0 + 0.18 * jax.random.normal(arg_keys[4], (C2,), jnp.float32), 0.1, 1.9),
        "conv_two": centred(arg_keys[5], (3, 3, 3, C2, C2), (27 * C2) ** -0.5, 0.078125),
        "frame_counts": draw_frame_counts(jax.random.fold_in(arg_keys[8], 71), 0),
        "row_counts": draw_row_counts(jax.random.fold_in(arg_keys[8], 71), 0),
    }


EPS = 1e-06

def rms_silu(values, gain):
    wide = values.astype(jnp.float32)
    factor = lax.rsqrt(lax.optimization_barrier(jnp.mean(wide * wide, axis=-1, keepdims=True)) + EPS)
    return jax.nn.silu(wide * factor * gain.astype(jnp.float32)).astype(jnp.bfloat16)

def row_tables(row_counts):
    total_rows = HS * N_ROWS
    row_index = jnp.arange(total_rows, dtype=jnp.int32)
    strip_of = row_index // HS
    slot_in = row_index % HS
    own_count = row_counts[strip_of]
    prior_count = row_counts[jnp.maximum(strip_of - 1, 0)]
    row_valid = slot_in < own_count
    upper_row = jnp.where(slot_in > 0, row_index - 1, (strip_of - 1) * HS + prior_count - 1)
    upper_valid = row_valid & ((slot_in > 0) | (strip_of > 0))
    lower_row = jnp.where(slot_in < own_count - 1, row_index + 1, (strip_of + 1) * HS)
    lower_valid = row_valid & ((slot_in < own_count - 1) | (strip_of < N_ROWS - 1))
    upper_row = jnp.clip(upper_row, 0, total_rows - 1).astype(jnp.int32)
    lower_row = jnp.clip(lower_row, 0, total_rows - 1).astype(jnp.int32)
    return (upper_row, upper_valid, lower_row, lower_valid, row_valid)

def row_planes(frames, tables):
    upper_row, upper_valid, lower_row, lower_valid, row_valid = tables
    blank = jnp.zeros_like(frames)
    above = jnp.where(upper_valid[None, :, None, None], jnp.take(frames, upper_row, axis=1), blank)
    below = jnp.where(lower_valid[None, :, None, None], jnp.take(frames, lower_row, axis=1), blank)
    return (above, frames, below)

def conv_planes(planes, weight, count):
    plane = planes[1]
    width = plane.shape[2]
    out_channels = weight.shape[-1]
    total = jnp.zeros((count * plane.shape[1] * width, out_channels), jnp.float32)
    for row_tap in range(3):
        padded = jnp.pad(planes[row_tap], ((0, 0), (0, 0), (1, 1), (0, 0)))
        for time_tap in range(3):
            for col_tap in range(3):
                window = padded[time_tap:time_tap + count, :, col_tap:col_tap + width]
                flat = window.reshape(-1, window.shape[-1])
                total = total + jnp.dot(flat, weight[time_tap, row_tap, col_tap], preferred_element_type=jnp.float32)
    return total.reshape(count, plane.shape[1], width, out_channels)

def reference(latents, gain_one, conv_one, up_weight, gain_two, conv_two, frame_counts, row_counts):
    height = HS * N_ROWS
    tables = row_tables(row_counts)
    row_valid = tables[4]
    act_one = rms_silu(latents, gain_one)
    padded_acts = jnp.concatenate([jnp.zeros((2,) + act_one.shape[1:], jnp.bfloat16), act_one], 0)

    def latent_step(frame_index):
        window = lax.dynamic_slice_in_dim(padded_acts, frame_index, 3, 0)
        conv = conv_planes(row_planes(window, tables), conv_one, 1)[0]
        source = lax.dynamic_index_in_dim(latents, frame_index, 0, keepdims=False)
        middle = (source.astype(jnp.float32) + conv).astype(jnp.bfloat16)
        paired = jnp.dot(middle.reshape(-1, C1), up_weight, preferred_element_type=jnp.float32)
        paired = jnp.transpose(paired.reshape(height, W, 2, C2), (2, 0, 1, 3))
        slot_ids = 2 * frame_index + jnp.arange(2, dtype=jnp.int32)
        live = slot_ids % FUP < frame_counts[slot_ids // FUP]
        keep = live[:, None, None, None] & row_valid[None, :, None, None]
        return jnp.where(keep, paired, 0.0).astype(jnp.bfloat16)
    upsampled = lax.map(latent_step, jnp.arange(LATENT_FRAMES, dtype=jnp.int32))
    upsampled = upsampled.reshape(SLOTS, height, W, C2)
    act_two = rms_silu(upsampled, gain_two)
    act_ext = jnp.concatenate([act_two, jnp.zeros((1,) + act_two.shape[1:], jnp.bfloat16)], 0)
    slot_index = jnp.arange(SLOTS, dtype=jnp.int32)
    live_slots = slot_index % FUP < frame_counts[slot_index // FUP]
    position = (jnp.cumsum(live_slots.astype(jnp.int32)) - 1).astype(jnp.int32)
    target = jnp.where(live_slots, position, SLOTS).astype(jnp.int32)
    table = jnp.full((SLOTS + 1,), SLOTS, jnp.int32).at[target].set(slot_index)
    table = table.at[SLOTS].set(SLOTS)
    before_one = jnp.where(live_slots & (position >= 1), table[jnp.maximum(position - 1, 0)], SLOTS).astype(jnp.int32)
    before_two = jnp.where(live_slots & (position >= 2), table[jnp.maximum(position - 2, 0)], SLOTS).astype(jnp.int32)

    def frame_step(slot_id):
        picks = jnp.stack([before_two[slot_id], before_one[slot_id], slot_id]).astype(jnp.int32)
        window = jnp.take(act_ext, picks, axis=0)
        conv = conv_planes(row_planes(window, tables), conv_two, 1)[0]
        source = lax.dynamic_index_in_dim(upsampled, slot_id, 0, keepdims=False)
        keep = live_slots[slot_id] & row_valid[:, None, None]
        return jnp.where(keep, source.astype(jnp.float32) + conv, 0.0).astype(jnp.bfloat16)
    return lax.map(frame_step, slot_index)
```

```python
import functools

import jax
import jax.numpy as jnp
from jax import lax
from jax.experimental import pallas as pl
from jax.experimental.pallas import tpu as pltpu
from jax.sharding import PartitionSpec as P

MESH = pl.DeviceIdType.MESH
EPS = 1e-06
BF = jnp.bfloat16
F32 = jnp.float32
N_MSG = 20


def rms_silu(wide, gain, scale):
    n = wide.shape[-1]
    mean = jnp.sum(wide * wide, axis=-1, keepdims=True) * (1.0 / n)
    half = wide * (lax.rsqrt(mean + EPS) * (0.5 * scale)) * gain
    return half * (1.0 + jnp.tanh(half))


def column_taps(act):
    width = act.shape[0]
    column = lax.broadcasted_iota(jnp.int32, act.shape, 0)
    left = jnp.where(column == 0, 0.0, pltpu.roll(act, 1, 0))
    right = jnp.where(column == width - 1, 0.0, pltpu.roll(act, width - 1, 0))
    return left, act, right


def kernel(
    n_tm, n_rows,
    frame_counts, row_counts, latents, gain_one, conv_one, up_weight, gain_two, conv_two,
    out,
    x_early, x_late, x_own, xlow, xup, xsend, act_one, w_one, acc_one, w_up_in, w_up,
    ubuf, ybuf, ylow, yup, ysend, m1_send, m2_send, tail_second, tail_last, act_two, w_two, acc_two, obuf,
    send_sem, recv_sem, load_sem, out_sem,
):
    t, r = lax.axis_index("tm"), lax.axis_index("rows")
    later, earlier = (lax.rem(t + 1, n_tm), r), (lax.rem(t + n_tm - 1, n_tm), r)
    lower, upper = (t, lax.rem(r + 1, n_rows)), (t, lax.rem(r + n_rows - 1, n_rows))
    row_count, frame_count = row_counts[r], frame_counts[t]
    last_row = jnp.maximum(row_count - 1, 0)
    strip, width, c1 = x_early.shape
    x_of = (x_early, x_late, x_own.at[0], x_own.at[1])
    tail_of = (tail_second, tail_last)
    c2 = ybuf.shape[-1]
    has_past = (t > 0).astype(F32)
    has_upper = (r > 0).astype(F32)
    has_lower = (r < n_rows - 1).astype(F32)

    def load(k, src, dst):
        return pltpu.make_async_copy(src, dst, load_sem.at[k])

    def message(k, src, dst, to):
        return pltpu.make_async_remote_copy(
            src_ref=src, dst_ref=dst, send_sem=send_sem.at[k], recv_sem=recv_sem.at[k],
            device_id=to, device_id_type=MESH,
        )

    own = load(0, latents, x_own)
    own.start()
    weights_one = {}
    for a in (2, 1, 0):
        for b in range(3):
            k = 1 + 3 * a + b
            weights_one[a, b] = load(
                k, conv_one.at[a, b], w_one.at[b, :, :, pl.ds((2 - a) * c1, c1)]
            )
    load_up = load(10, up_weight, w_up_in)
    weights_two = [
        load(11 + 3 * a + b, conv_two.at[a, b], w_two.at[a, b, pl.ds(0, 3 * c2)]) for a in range(3) for b in range(3)
    ]

    barrier = pltpu.get_barrier_semaphore()
    for place in (later, earlier, lower, upper):
        pl.semaphore_signal(barrier, inc=1, device_id=place, device_id_type=MESH)
    for a in (2, 1, 0):
        for b in range(3):
            weights_one[a, b].start()
    load_up.start()
    for copy in weights_two:
        copy.start()
    pl.semaphore_wait(barrier, 4)

    frame_late = message(0, latents.at[1], x_late, later)
    frame_early = [
        message(1, latents.at[0, 3:8], x_early.at[3:8], later),
        message(2, latents.at[0, 0:1], x_early.at[0:1], later),
        message(3, latents.at[0, 1:3], x_early.at[1:3], later),
    ]
    rim_first = message(4, latents.at[:, 0], xlow.at[2:4], upper)
    rim_last = message(5, xsend.at[2:4], xup.at[2:4], lower)
    rim_first.start()
    frame_late.start()
    for copy in frame_early:
        copy.start()
    own.wait()
    for f in (2, 3):
        xsend[f] = x_of[f][last_row]
    rim_last.start()

    gain_1 = gain_one[...].reshape(1, c1)
    gain_2 = gain_two[...].reshape(1, c2)

    def pack_one(f, first, last, past):
        def step(s, _):
            is_upper, is_lower = s == 0, (s == strip + 1) | (s - 1 == row_count)
            mine = x_of[f][jnp.clip(s - 1, 0, strip - 1)]
            raw = lax.select(is_upper, xup[f], lax.select(is_lower, xlow[f], mine))
            scale = past * jnp.where(is_upper, has_upper, jnp.where(is_lower, has_lower, 1.0))
            taps = column_taps(rms_silu(raw.astype(F32), gain_1, scale))
            for e in range(3):
                act_one[f, s, :, e * c1 : (e + 1) * c1] = taps[e].astype(BF)
            return 0

        lax.fori_loop(first, last, step, 0)

    def pack_inner(f, first, last, past):
        def step(s, _):
            taps = column_taps(rms_silu(x_of[f][s - 1].astype(F32), gain_1, past))
            for e in range(3):
                act_one[f, s, :, e * c1 : (e + 1) * c1] = taps[e].astype(BF)
            return 0

        lax.fori_loop(first, last, step, 0)

    def conv_one_dot(f, row, rows, first, last):
        planes = [act_one[f, row + b : row + b + rows].reshape(rows * width, 3 * c1) for b in range(3)]
        weight = w_one[:, :, :, first * c1 : last * c1].reshape(9 * c1, (last - first) * c1)
        return jnp.dot(jnp.concatenate(planes, axis=1), weight, preferred_element_type=F32)

    for f in (2, 3):
        pack_inner(f, 1, 5, 1.0)
    rim_first.wait_recv()
    rim_last.wait_recv()
    for f in (2, 3):
        pack_one(f, 0, 1, 1.0)
        pack_one(f, 5, 10, 1.0)

    for a in (2, 1):
        for b in range(3):
            weights_one[a, b].wait()
    acc_one[...] = conv_one_dot(2, 0, strip, 0, 2)
    acc_one[:, c1 : 2 * c1] += conv_one_dot(3, 0, strip, 0, 1)
    for b in range(3):
        weights_one[0, b].wait()
    load_up.wait()
    w_up[...] = jnp.zeros_like(w_up)
    w_up[:, 0:c2] = w_up_in[:, 0:c2]
    w_up[:, 256 : 256 + c2] = w_up_in[:, c2 : 2 * c2]

    def forward_rims_one(k, f):
        xsend[f] = x_of[f][last_row]
        first = message(k, x_of[f].at[0], xlow.at[f], upper)
        final = message(k + 1, xsend.at[f], xup.at[f], lower)
        first.start()
        final.start()
        return first, final

    frame_late.wait_recv()
    late_rims = forward_rims_one(6, 1)
    pack_inner(1, 1, 5, has_past)
    for copy in late_rims:
        copy.wait_recv()
    pack_one(1, 0, 1, has_past)
    pack_one(1, 5, 10, has_past)
    acc_one[...] += conv_one_dot(1, 0, strip, 1, 3)

    for copy in weights_two:
        copy.wait()
    w_two[:, :, 3 * c2 :] = jnp.zeros((3, 3, 64, c2), BF)

    def live(slot, row):
        return ((slot < frame_count) & (row < row_count)).astype(F32)

    def middle_rows(row, rows):
        cells = pl.ds(row * width, rows * width)
        acc_one[cells, 0:c1] += conv_one_dot(0, row, rows, 2, 3)
        for f in range(2):
            wide = x_own[f, row : row + rows].reshape(rows * width, c1).astype(F32)
            mid = (wide + acc_one[cells, f * c1 : (f + 1) * c1]).astype(BF)
            pair = jnp.dot(mid, w_up[...], preferred_element_type=F32)
            for s in range(2):
                half = pair[:, 256 * s : 256 * s + c2].astype(BF)
                ubuf[2 * f + s, row : row + rows] = half.reshape(rows, width, c2)

        def step(k, _):
            slot, place = k // rows, row + k % rows
            wide = ubuf[slot, place].astype(F32) * live(slot, place)
            ubuf[slot, place] = wide.astype(BF)
            ybuf[slot, place] = rms_silu(wide, gain_2, 1.0).astype(BF)
            return 0

        lax.fori_loop(0, 4 * rows, step, 0)

    def send_last(k, row, rows):
        def step(place, _):
            m1_send[place] = ybuf[jnp.maximum(frame_count - 1, 0), place]
            return 0

        lax.fori_loop(row, row + rows, step, 0)
        copy = message(k, m1_send.at[row : row + rows], tail_last.at[row : row + rows], later)
        copy.start()
        return copy

    def send_second(k, row, rows):
        def step(place, _):
            second = ybuf[jnp.maximum(frame_count - 2, 0), place]
            passed = (tail_last[place].astype(F32) * has_past).astype(BF)
            m2_send[place] = lax.select(frame_count >= 2, second, passed)
            return 0

        lax.fori_loop(row, row + rows, step, 0)
        copy = message(k, m2_send.at[row : row + rows], tail_second.at[row : row + rows], later)
        copy.start()
        return copy

    half_rows = strip // 2
    for copy in frame_early:
        copy.wait_recv()
    early_rims = forward_rims_one(8, 0)
    pack_inner(0, 1, 5, has_past)
    for copy in early_rims:
        copy.wait_recv()
    pack_one(0, 0, 1, has_past)
    pack_one(0, 5, 10, has_past)
    middle_rows(half_rows, half_rows)
    last_b = send_last(12, half_rows, half_rows)
    middle_rows(0, half_rows)
    last_a = send_last(13, 0, half_rows)

    for f in range(4):
        ysend[2 + f] = ybuf[f, last_row]
    two_first = message(10, ybuf.at[:, 0], ylow.at[2:6], upper)
    two_last = message(11, ysend.at[2:6], yup.at[2:6], lower)
    two_first.start()
    two_last.start()

    def pack_two(f, first, last, past, rows_of):
        def step(s, _):
            is_upper, is_lower = s == 0, (s == strip + 1) | (s - 1 == row_count)
            mine = rows_of(jnp.clip(s - 1, 0, strip - 1))
            raw = lax.select(is_upper, yup[f], lax.select(is_lower, ylow[f], mine))
            scale = past * jnp.where(is_upper, has_upper, jnp.where(is_lower, has_lower, 1.0))
            left, middle, right = column_taps(raw.astype(F32) * scale)
            blank = jnp.zeros((width, 640 - 3 * c2), F32)
            row = jnp.concatenate([left, middle, right, blank], axis=1)
            act_two[f, s] = row.astype(BF)
            return 0

        lax.fori_loop(first, last, step, 0)

    two_first.wait_recv()
    two_last.wait_recv()
    for f in range(4):
        pack_two(2 + f, 0, strip + 2, 1.0, lambda place, f=f: ybuf[f, place])

    last_b.wait_recv()
    second_b = send_second(14, half_rows, half_rows)
    last_a.wait_recv()
    second_a = send_second(15, 0, half_rows)

    def forward_rims_two(k, f):
        ysend[f] = tail_of[f][last_row]
        first = message(k, tail_of[f].at[0], ylow.at[f], upper)
        final = message(k + 1, ysend.at[f], yup.at[f], lower)
        first.start()
        final.start()
        return first, final

    rims_last = forward_rims_two(16, 1)

    def conv_two_dot(frames, taps):
        planes = [
            act_two[f, b : b + strip].reshape(strip * width, 640) for f in frames for b in range(3)
        ]
        weight = w_two[taps[0] : taps[-1] + 1].reshape(len(taps) * 3 * 640, c2)
        return jnp.dot(jnp.concatenate(planes, axis=1), weight, preferred_element_type=F32)

    def finish(q):
        def step(place, _):
            wide = ubuf[q, place].astype(F32)
            conv = acc_two[q % 2, pl.ds(pl.multiple_of(place * width, width), width)]
            obuf[q, place] = ((wide + conv) * live(q, place)).astype(BF)
            return 0

        lax.fori_loop(0, strip, step, 0)
        copy = pltpu.make_async_copy(obuf.at[q], out.at[q], out_sem.at[q])
        copy.start()
        return copy

    written = []
    for q in (3, 2):
        acc_two[q % 2] = conv_two_dot((q, q + 1, q + 2), (0, 1, 2))
        written.append(finish(q))
    acc_two[1] = conv_two_dot((2, 3), (1, 2))
    acc_two[0] = conv_two_dot((2,), (2,))

    for copy in rims_last:
        copy.wait_recv()
    pack_two(1, 0, strip + 2, has_past, lambda place: tail_last[place])
    acc_two[1] += conv_two_dot((1,), (0,))
    written.append(finish(1))
    second_b.wait_recv()
    second_a.wait_recv()
    rims_second = forward_rims_two(18, 0)
    for copy in rims_second:
        copy.wait_recv()
    pack_two(0, 0, strip + 2, has_past, lambda place: tail_second[place])
    acc_two[0] += conv_two_dot((0, 1), (0, 1))
    written.append(finish(0))

    sent = [frame_late, *frame_early, rim_first, rim_last, *late_rims, *early_rims, last_b, last_a]
    sent += [two_first, two_last, second_b, second_a, *rims_last, *rims_second]
    for copy in sent:
        copy.wait_send()
    for copy in written:
        copy.wait()


def on_device(n_tm, n_rows, latents, gain_one, conv_one, up_weight, gain_two, conv_two, frame_counts, row_counts):
    frames, strip, width, c1 = latents.shape
    c2 = gain_two.shape[0]
    slots = 2 * frames
    cells = strip * width
    vmem = pltpu.VMEM
    scratch = [
        vmem((strip, width, c1), BF),
        vmem((strip, width, c1), BF),
        vmem((2, strip, width, c1), BF),
        vmem((4, width, c1), BF),
        vmem((4, width, c1), BF),
        vmem((4, width, c1), BF),
        vmem((4, strip + 2, width, 3 * c1), BF),
        vmem((3, 3, c1, 3 * c1), BF),
        vmem((cells, 2 * c1), F32),
        vmem((c1, 2 * c2), BF),
        vmem((c1, 512), BF),
        vmem((slots, strip, width, c2), BF),
        vmem((slots, strip, width, c2), BF),
        vmem((6, width, c2), BF),
        vmem((6, width, c2), BF),
        vmem((6, width, c2), BF),
        vmem((strip, width, c2), BF),
        vmem((strip, width, c2), BF),
        vmem((strip, width, c2), BF),
        vmem((strip, width, c2), BF),
        vmem((6, strip + 2, width, 640), BF),
        vmem((3, 3, 3 * c2 + 64, c2), BF),
        vmem((2, cells, c2), F32),
        vmem((slots, strip, width, c2), BF),
        pltpu.SemaphoreType.DMA((N_MSG,)),
        pltpu.SemaphoreType.DMA((N_MSG,)),
        pltpu.SemaphoreType.DMA((20,)),
        pltpu.SemaphoreType.DMA((4,)),
    ]
    smem, anywhere = pl.BlockSpec(memory_space=pltpu.SMEM), pl.BlockSpec(memory_space=pl.ANY)
    in_vmem = pl.BlockSpec(memory_space=pltpu.VMEM)
    return pl.pallas_call(
        functools.partial(kernel, n_tm, n_rows),
        out_shape=jax.ShapeDtypeStruct((slots, strip, width, c2), BF),
        in_specs=[smem, smem, anywhere, in_vmem, anywhere, anywhere, in_vmem, anywhere],
        out_specs=anywhere,
        scratch_shapes=scratch,
        compiler_params=pltpu.CompilerParams(
            collective_id=0, has_side_effects=True, vmem_limit_bytes=60 * 2**20
        ),
    )(frame_counts, row_counts, latents, gain_one, conv_one, up_weight, gain_two, conv_two.reshape(3, 3, 3 * c2, c2))


def solution(mesh):
    in_specs = (P("tm", "rows", None, None), P(), P(), P(), P(), P(), P(), P())
    return jax.shard_map(
        functools.partial(on_device, mesh.shape["tm"], mesh.shape["rows"]),
        mesh=mesh, in_specs=in_specs, out_specs=P("tm", "rows", None, None), check_vma=False,
    )
```

```python
import functools

import jax
import jax.numpy as jnp
from jax import lax
from jax.experimental import pallas as pl
from jax.experimental.pallas import tpu as pltpu
from jax.sharding import PartitionSpec as P

MESH = pl.DeviceIdType.MESH
EPS = 1e-06
BF = jnp.bfloat16
F32 = jnp.float32
N_MSG = 22
CHUNKS = ((4, 4), (0, 4))


def rms_silu(wide, gain, scale):
    n = wide.shape[-1]
    mean = jnp.sum(wide * wide, axis=-1, keepdims=True) * (1.0 / n)
    half = wide * (lax.rsqrt(mean + EPS) * (0.5 * scale)) * gain
    return half * (1.0 + jnp.tanh(half))


def column_taps(act):
    width = act.shape[0]
    column = lax.broadcasted_iota(jnp.int32, act.shape, 0)
    left = jnp.where(column == 0, 0.0, pltpu.roll(act, 1, 0))
    right = jnp.where(column == width - 1, 0.0, pltpu.roll(act, width - 1, 0))
    return left, act, right


def kernel(
    n_tm, n_rows,
    frame_counts, row_counts, latents, gain_one, conv_one, up_weight, gain_two, conv_two,
    out,
    q_send, q_recv, x_late, x_own, xlow, xup, xsend, act_one, w_one, acc_one, w_up_in, w_up,
    ubuf, ybuf, ylow, yup, low_last, up_last, low_second, up_second, rim_send, ysend, m1_send, m2_send, tail_second, tail_last, act_two, w_two, acc_two, obuf,
    send_sem, recv_sem, load_sem, out_sem,
):
    t, r = lax.axis_index("tm"), lax.axis_index("rows")
    later, earlier = (lax.rem(t + 1, n_tm), r), (lax.rem(t + n_tm - 1, n_tm), r)
    lower, upper = (t, lax.rem(r + 1, n_rows)), (t, lax.rem(r + n_rows - 1, n_rows))
    row_count, frame_count = row_counts[r], frame_counts[t]
    last_row = jnp.maximum(row_count - 1, 0)
    strip, width, c1 = x_late.shape
    x_of = (None, x_late, x_own.at[0], x_own.at[1])
    tail_of = (tail_second, tail_last)
    up_of = (up_second, up_last, *(yup.at[f] for f in range(4)))
    low_of = (low_second, low_last, *(ylow.at[f] for f in range(4)))
    c2 = ybuf.shape[-1]
    has_past = (t > 0).astype(F32)
    has_upper = (r > 0).astype(F32)
    has_lower = (r < n_rows - 1).astype(F32)

    def load(k, src, dst):
        return pltpu.make_async_copy(src, dst, load_sem.at[k])

    def message(k, src, dst, to):
        return pltpu.make_async_remote_copy(
            src_ref=src, dst_ref=dst, send_sem=send_sem.at[k], recv_sem=recv_sem.at[k],
            device_id=to, device_id_type=MESH,
        )

    own = load(0, latents, x_own)
    own.start()
    weights_one = {}
    for a in (2, 1, 0):
        for b in range(3):
            k = 1 + 3 * a + b
            weights_one[a, b] = load(
                k, conv_one.at[a, b], w_one.at[b, :, :, pl.ds((2 - a) * c1, c1)]
            )
    load_up = load(10, up_weight, w_up_in)
    weights_two = [
        load(11 + 3 * a + b, conv_two.at[a, b], w_two.at[a, b, pl.ds(0, 3 * c2)]) for a in range(3) for b in range(3)
    ]

    barrier = pltpu.get_barrier_semaphore()
    for place in (later, earlier, lower, upper):
        pl.semaphore_signal(barrier, inc=1, device_id=place, device_id_type=MESH)
    for a in (0, 2, 1):
        for b in range(3):
            weights_one[a, b].start()
    load_up.start()
    for copy in weights_two:
        copy.start()
    pl.semaphore_wait(barrier, 4)

    halves = strip // 2
    received = [
        message(i, latents.at[1, first:last], x_late.at[first:last], later)
        for i, (first, last) in enumerate(((0, 1), (halves - 1, strip), (1, halves - 1)))
    ]
    rim_first = message(6, latents.at[:, 0], xlow.at[2:4], upper)
    rim_last = message(7, xsend.at[2:4], xup.at[2:4], lower)
    rim_first.start()
    for copy in received:
        copy.start()
    own.wait()
    for f in (2, 3):
        xsend[f] = x_of[f][last_row]
    rim_last.start()

    gain_1 = gain_one[...].reshape(1, c1)
    gain_2 = gain_two[...].reshape(1, c2)

    def pack_one(f, first, last, past):
        def step(s, _):
            is_upper, is_lower = s == 0, (s == strip + 1) | (s - 1 == row_count)
            mine = x_of[f][jnp.clip(s - 1, 0, strip - 1)]
            raw = lax.select(is_upper, xup[f], lax.select(is_lower, xlow[f], mine))
            scale = past * jnp.where(is_upper, has_upper, jnp.where(is_lower, has_lower, 1.0))
            taps = column_taps(rms_silu(raw.astype(F32), gain_1, scale))
            for e in range(3):
                act_one[f, s, :, e * c1 : (e + 1) * c1] = taps[e].astype(BF)
            return 0

        lax.fori_loop(first, last, step, 0, unroll=True)

    def pack_inner(f, first, last, past):
        def step(s, _):
            taps = column_taps(rms_silu(x_of[f][s - 1].astype(F32), gain_1, past))
            for e in range(3):
                act_one[f, s, :, e * c1 : (e + 1) * c1] = taps[e].astype(BF)
            return 0

        lax.fori_loop(first, last, step, 0, unroll=True)

    def conv_one_dot(f, row, rows, first, last):
        planes = [act_one[f, row + b : row + b + rows].reshape(rows * width, 3 * c1) for b in range(3)]
        weight = w_one[:, :, :, first * c1 : last * c1].reshape(9 * c1, (last - first) * c1)
        return jnp.dot(jnp.concatenate(planes, axis=1), weight, preferred_element_type=F32)

    for f in (2, 3):
        pack_inner(f, 1, 5, 1.0)
    rim_first.wait_recv()
    rim_last.wait_recv()
    for f in (2, 3):
        pack_one(f, 0, 1, 1.0)
        pack_one(f, 5, 10, 1.0)

    for b in range(3):
        weights_one[0, b].wait()
    q_send[...] = conv_one_dot(2, 0, strip, 2, 3).astype(BF).reshape(strip, width, c1)
    shares = []
    for i, (row, rows) in enumerate(CHUNKS):
        shares.append(message(3 + i, q_send.at[row : row + rows], q_recv.at[row : row + rows], later))
        shares[i].start()
    for a in (2, 1):
        for b in range(3):
            weights_one[a, b].wait()
    acc_one[...] = conv_one_dot(2, 0, strip, 0, 2)
    def pick_last(rows):
        row = rows[halves - 1]
        for place in range(halves, strip):
            row = lax.select(last_row == place, rows[place], row)
        return row

    received[0].wait_recv()
    received[1].wait_recv()
    xsend[1] = pick_last(x_late)
    late_rims = [message(8, x_late.at[0], xlow.at[1], upper), message(9, xsend.at[1], xup.at[1], lower)]
    for copy in late_rims:
        copy.start()
    acc_one[:, c1 : 2 * c1] += conv_one_dot(3, 0, strip, 0, 1)
    load_up.wait()
    w_up[...] = jnp.zeros_like(w_up)
    w_up[:, 0:c2] = w_up_in[:, 0:c2]
    w_up[:, 256 : 256 + c2] = w_up_in[:, c2 : 2 * c2]
    received[2].wait_recv()
    pack_inner(1, 1, halves + 1, has_past)
    for copy in late_rims:
        copy.wait_recv()
    pack_one(1, 0, 1, has_past)
    pack_one(1, halves + 1, strip + 2, has_past)
    acc_one[...] += conv_one_dot(1, 0, strip, 1, 3)

    for copy in weights_two:
        copy.wait()
    w_two[:, :, 3 * c2 :] = jnp.zeros((3, 3, 64, c2), BF)

    def live(slot, row):
        return ((slot < frame_count) & (row < row_count)).astype(F32)

    def middle_rows(row, rows):
        cells = pl.ds(row * width, rows * width)
        for f in range(2):
            wide = x_own[f, row : row + rows].reshape(rows * width, c1).astype(F32)
            wide = wide + acc_one[cells, f * c1 : (f + 1) * c1]
            if f == 0:
                wide = wide + q_recv[row : row + rows].reshape(rows * width, c1).astype(F32) * has_past
            mid = wide.astype(BF)
            pair = jnp.dot(mid, w_up[...], preferred_element_type=F32)
            for s in range(2):
                half = pair[:, 256 * s : 256 * s + c2].astype(BF)
                ubuf[2 * f + s, row : row + rows] = half.reshape(rows, width, c2)

        def step(k, _):
            slot, place = k // rows, row + k % rows
            wide = ubuf[slot, place].astype(F32) * live(slot, place)
            ubuf[slot, place] = wide.astype(BF)
            ybuf[slot, place] = rms_silu(wide, gain_2, 1.0).astype(BF)
            return 0

        lax.fori_loop(0, 4 * rows, step, 0, unroll=4 * rows if rows < 4 else 8)

    def send_last(k, row, rows):
        def step(place, _):
            m1_send[place] = ybuf[jnp.maximum(frame_count - 1, 0), place]
            return 0

        lax.fori_loop(row, row + rows, step, 0, unroll=True)
        copy = message(k, m1_send.at[row : row + rows], tail_last.at[row : row + rows], later)
        copy.start()
        return copy

    def send_second(k, row, rows):
        def step(place, _):
            second = ybuf[jnp.maximum(frame_count - 2, 0), place]
            passed = (tail_last[place].astype(F32) * has_past).astype(BF)
            m2_send[place] = lax.select(frame_count >= 2, second, passed)
            return 0

        lax.fori_loop(row, row + rows, step, 0, unroll=True)
        copy = message(k, m2_send.at[row : row + rows], tail_second.at[row : row + rows], later)
        copy.start()
        return copy

    last = []
    for i, (row, rows) in enumerate(CHUNKS):
        shares[i].wait_recv()
        middle_rows(row, rows)
        last.append(send_last(12 + i, row, rows))

    for f in range(4):
        ysend[f] = ybuf[f, last_row]
    two_first = message(10, ybuf.at[:, 0], ylow, upper)
    two_last = message(11, ysend.at[0:4], yup, lower)
    two_first.start()
    two_last.start()

    def taps_two(f, s, raw, scale):
        left, middle, right = column_taps(raw.astype(F32) * scale)
        blank = jnp.zeros((width, 640 - 3 * c2), F32)
        act_two[f, s] = jnp.concatenate([left, middle, right, blank], axis=1).astype(BF)

    def pack_two(f, first, last, past, rows_of):
        def step(s, _):
            is_upper, is_lower = s == 0, (s == strip + 1) | (s - 1 == row_count)
            mine = rows_of(jnp.clip(s - 1, 0, strip - 1))
            raw = lax.select(is_upper, up_of[f][...], lax.select(is_lower, low_of[f][...], mine))
            scale = past * jnp.where(is_upper, has_upper, jnp.where(is_lower, has_lower, 1.0))
            taps_two(f, s, raw, scale)
            return 0

        lax.fori_loop(first, last, step, 0, unroll=True)

    def pack_two_inner(f, first, last, past, rows_of):
        def step(s, _):
            taps_two(f, s, rows_of(s - 1), past)
            return 0

        lax.fori_loop(first, last, step, 0, unroll=True)

    def rows_of(f):
        return lambda place: ybuf[f, place]

    def conv_two_dot(frames, taps):
        planes = [
            act_two[f, b : b + strip].reshape(strip * width, 640) for f in frames for b in range(3)
        ]
        weight = w_two[taps[0] : taps[-1] + 1].reshape(len(taps) * 3 * 640, c2)
        return jnp.dot(jnp.concatenate(planes, axis=1), weight, preferred_element_type=F32)

    def finish(q):
        def step(place, _):
            wide = ubuf[q, place].astype(F32)
            conv = acc_two[q % 2, pl.ds(pl.multiple_of(place * width, width), width)]
            obuf[q, place] = ((wide + conv) * live(q, place)).astype(BF)
            return 0

        lax.fori_loop(0, strip, step, 0, unroll=True)
        copy = pltpu.make_async_copy(obuf.at[q], out.at[q], out_sem.at[q])
        copy.start()
        return copy

    def pack_tail(f):
        of = lambda place: tail_of[f][place]
        pack_two(f, 0, 1, has_past, of)
        pack_two_inner(f, 1, halves + 1, has_past, of)
        pack_two(f, halves + 1, strip + 2, has_past, of)

    written, second = [], []
    for f in range(4):
        pack_two_inner(2 + f, 1, halves + 1, 1.0, rows_of(f))
    for i, (row, rows) in enumerate(CHUNKS[:-1]):
        last[i].wait_recv()
        second.append(send_second(15 + i, row, rows))
    two_first.wait_recv()
    two_last.wait_recv()
    for f in range(4):
        pack_two(2 + f, 0, 1, 1.0, rows_of(f))
        pack_two(2 + f, halves + 1, strip + 2, 1.0, rows_of(f))
    acc_two[1] = conv_two_dot((3, 4, 5), (0, 1, 2))
    last[-1].wait_recv()
    second.append(send_second(15 + len(CHUNKS) - 1, *CHUNKS[-1]))
    ysend[4] = pick_last(tail_last)
    rims_last = [message(18, tail_last.at[0], low_last, upper), message(19, ysend.at[4], up_last, lower)]
    for copy in rims_last:
        copy.start()
    written.append(finish(3))
    acc_two[0] = conv_two_dot((2, 3, 4), (0, 1, 2))
    written.append(finish(2))
    for copy in rims_last:
        copy.wait_recv()
    own_second = jnp.maximum(frame_count - 2, 0)
    for i, (of, passed) in enumerate(((yup, up_last), (ylow, low_last))):
        passed = (passed[...].astype(F32) * has_past).astype(BF)
        rim_send[i] = lax.select(frame_count >= 2, of[own_second], passed)
    rims_second = [message(20, rim_send.at[0], up_second, later), message(21, rim_send.at[1], low_second, later)]
    for copy in rims_second:
        copy.start()
    pack_tail(1)
    acc_two[1] = conv_two_dot((1, 2, 3), (0, 1, 2))
    written.append(finish(1))
    acc_two[0] = conv_two_dot((1, 2), (1, 2))
    for copy in (*second, *rims_second):
        copy.wait_recv()
    pack_tail(0)
    acc_two[0] += conv_two_dot((0,), (0,))
    written.append(finish(0))

    sent = [*received, rim_first, rim_last, *shares, *late_rims, *last]
    sent += [two_first, two_last, *second, *rims_last, *rims_second]
    for copy in sent:
        copy.wait_send()
    for copy in written:
        copy.wait()


def on_device(n_tm, n_rows, latents, gain_one, conv_one, up_weight, gain_two, conv_two, frame_counts, row_counts):
    frames, strip, width, c1 = latents.shape
    c2 = gain_two.shape[0]
    slots = 2 * frames
    cells = strip * width
    vmem = pltpu.VMEM
    scratch = [
        vmem((strip, width, c1), BF),
        vmem((strip, width, c1), BF),
        vmem((strip, width, c1), BF),
        vmem((2, strip, width, c1), BF),
        vmem((4, width, c1), BF),
        vmem((4, width, c1), BF),
        vmem((4, width, c1), BF),
        vmem((4, strip + 2, width, 3 * c1), BF),
        vmem((3, 3, c1, 3 * c1), BF),
        vmem((cells, 2 * c1), F32),
        vmem((c1, 2 * c2), BF),
        vmem((c1, 512), BF),
        vmem((slots, strip, width, c2), BF),
        vmem((slots, strip, width, c2), BF),
        vmem((4, width, c2), BF),
        vmem((4, width, c2), BF),
        vmem((width, c2), BF),
        vmem((width, c2), BF),
        vmem((width, c2), BF),
        vmem((width, c2), BF),
        vmem((2, width, c2), BF),
        vmem((5, width, c2), BF),
        vmem((strip, width, c2), BF),
        vmem((strip, width, c2), BF),
        vmem((strip, width, c2), BF),
        vmem((strip, width, c2), BF),
        vmem((6, strip + 2, width, 640), BF),
        vmem((3, 3, 3 * c2 + 64, c2), BF),
        vmem((2, cells, c2), F32),
        vmem((slots, strip, width, c2), BF),
        pltpu.SemaphoreType.DMA((N_MSG,)),
        pltpu.SemaphoreType.DMA((N_MSG,)),
        pltpu.SemaphoreType.DMA((20,)),
        pltpu.SemaphoreType.DMA((4,)),
    ]
    smem, anywhere = pl.BlockSpec(memory_space=pltpu.SMEM), pl.BlockSpec(memory_space=pl.ANY)
    in_vmem = pl.BlockSpec(memory_space=pltpu.VMEM)
    return pl.pallas_call(
        functools.partial(kernel, n_tm, n_rows),
        out_shape=jax.ShapeDtypeStruct((slots, strip, width, c2), BF),
        in_specs=[smem, smem, anywhere, in_vmem, anywhere, anywhere, in_vmem, anywhere],
        out_specs=anywhere,
        scratch_shapes=scratch,
        compiler_params=pltpu.CompilerParams(
            collective_id=0, has_side_effects=True, vmem_limit_bytes=60 * 2**20
        ),
    )(frame_counts, row_counts, latents, gain_one, conv_one, up_weight, gain_two, conv_two.reshape(3, 3, 3 * c2, c2))


def solution(mesh):
    in_specs = (P("tm", "rows", None, None), P(), P(), P(), P(), P(), P(), P())
    return jax.shard_map(
        functools.partial(on_device, mesh.shape["tm"], mesh.shape["rows"]),
        mesh=mesh, in_specs=in_specs, out_specs=P("tm", "rows", None, None), check_vma=False,
    )
```

```python
import functools

import jax
import jax.numpy as jnp
from jax import lax
from jax.experimental import pallas as pl
from jax.experimental.pallas import tpu as pltpu
from jax.sharding import PartitionSpec as P

MESH = pl.DeviceIdType.MESH
EPS = 1e-06
BF = jnp.bfloat16
F32 = jnp.float32
N_MSG = 22
CHUNKS = ((4, 4), (0, 4))


def rms_silu(wide, gain, scale):
    n = wide.shape[-1]
    mean = jnp.sum(wide * wide, axis=-1, keepdims=True) * (1.0 / n)
    half = wide * (lax.rsqrt(mean + EPS) * (0.5 * scale)) * gain
    return half * (1.0 + jnp.tanh(half))


def column_taps(act):
    width = act.shape[0]
    column = lax.broadcasted_iota(jnp.int32, act.shape, 0)
    left = jnp.where(column == 0, 0.0, pltpu.roll(act, 1, 0))
    right = jnp.where(column == width - 1, 0.0, pltpu.roll(act, width - 1, 0))
    return left, act, right


def kernel(
    n_tm, n_rows,
    frame_counts, row_counts, latents, gain_one, conv_one, up_weight, gain_two, conv_two,
    out,
    q_send, q_recv, x_late, x_own, xlow, xup, xsend, act_one, w_one, acc_one, w_up_in, w_up,
    ubuf, ybuf, ylow, yup, low_last, up_last, low_second, up_second, rim_send, ysend, m1_send, m2_send, tail_second, tail_last, act_two, w_two, acc_two,
    send_sem, recv_sem, load_sem,
):
    t, r = lax.axis_index("tm"), lax.axis_index("rows")
    later, earlier = (lax.rem(t + 1, n_tm), r), (lax.rem(t + n_tm - 1, n_tm), r)
    lower, upper = (t, lax.rem(r + 1, n_rows)), (t, lax.rem(r + n_rows - 1, n_rows))
    row_count, frame_count = row_counts[r], frame_counts[t]
    last_row = jnp.maximum(row_count - 1, 0)
    strip, width, c1 = x_late.shape
    x_of = (None, x_late, x_own.at[0], x_own.at[1])
    tail_of = (tail_second, tail_last)
    up_of = (up_second, up_last, *(yup.at[f] for f in range(4)))
    low_of = (low_second, low_last, *(ylow.at[f] for f in range(4)))
    c2 = ybuf.shape[-1]
    has_past = (t > 0).astype(F32)
    has_upper = (r > 0).astype(F32)
    has_lower = (r < n_rows - 1).astype(F32)

    def load(k, src, dst):
        return pltpu.make_async_copy(src, dst, load_sem.at[k])

    def message(k, src, dst, to):
        return pltpu.make_async_remote_copy(
            src_ref=src, dst_ref=dst, send_sem=send_sem.at[k], recv_sem=recv_sem.at[k],
            device_id=to, device_id_type=MESH,
        )

    own = load(0, latents, x_own)
    own.start()
    weights_one = {}
    for a in (2, 1, 0):
        for b in range(3):
            k = 1 + 3 * a + b
            weights_one[a, b] = load(
                k, conv_one.at[a, b], w_one.at[b, :, :, pl.ds((2 - a) * c1, c1)]
            )
    load_up = load(10, up_weight, w_up_in)
    weights_two = [
        load(11 + 3 * a + b, conv_two.at[a, b], w_two.at[a, b, pl.ds(0, 3 * c2)]) for a in range(3) for b in range(3)
    ]

    barrier = pltpu.get_barrier_semaphore()
    for place in (later, earlier, lower, upper):
        pl.semaphore_signal(barrier, inc=1, device_id=place, device_id_type=MESH)
    for a in (0, 2, 1):
        for b in range(3):
            weights_one[a, b].start()
    load_up.start()
    for copy in weights_two:
        copy.start()
    pl.semaphore_wait(barrier, 4)

    halves = strip // 2
    received = [
        message(i, latents.at[1, first:last], x_late.at[first:last], later)
        for i, (first, last) in enumerate(((0, 1), (halves - 1, strip), (1, halves - 1)))
    ]
    rim_first = message(6, latents.at[:, 0], xlow.at[2:4], upper)
    rim_last = message(7, xsend.at[2:4], xup.at[2:4], lower)
    rim_first.start()
    for copy in received:
        copy.start()
    own.wait()
    for f in (2, 3):
        xsend[f] = x_of[f][last_row]
    rim_last.start()

    gain_1 = gain_one[...].reshape(1, c1)
    gain_2 = gain_two[...].reshape(1, c2)

    def pack_one(f, first, last, past):
        def step(s, _):
            is_upper, is_lower = s == 0, (s == strip + 1) | (s - 1 == row_count)
            mine = x_of[f][jnp.clip(s - 1, 0, strip - 1)]
            raw = lax.select(is_upper, xup[f], lax.select(is_lower, xlow[f], mine))
            scale = past * jnp.where(is_upper, has_upper, jnp.where(is_lower, has_lower, 1.0))
            taps = column_taps(rms_silu(raw.astype(F32), gain_1, scale))
            for e in range(3):
                act_one[f, s, :, e * c1 : (e + 1) * c1] = taps[e].astype(BF)
            return 0

        lax.fori_loop(first, last, step, 0, unroll=True)

    def pack_inner(f, first, last, past):
        def step(s, _):
            taps = column_taps(rms_silu(x_of[f][s - 1].astype(F32), gain_1, past))
            for e in range(3):
                act_one[f, s, :, e * c1 : (e + 1) * c1] = taps[e].astype(BF)
            return 0

        lax.fori_loop(first, last, step, 0, unroll=True)

    def conv_one_dot(f, row, rows, first, last):
        planes = [act_one[f, row + b : row + b + rows].reshape(rows * width, 3 * c1) for b in range(3)]
        weight = w_one[:, :, :, first * c1 : last * c1].reshape(9 * c1, (last - first) * c1)
        return jnp.dot(jnp.concatenate(planes, axis=1), weight, preferred_element_type=F32)

    for f in (2, 3):
        pack_inner(f, 1, 5, 1.0)
    rim_first.wait_recv()
    rim_last.wait_recv()
    for f in (2, 3):
        pack_one(f, 0, 1, 1.0)
        pack_one(f, 5, 10, 1.0)

    for b in range(3):
        weights_one[0, b].wait()
    q_send[...] = conv_one_dot(2, 0, strip, 2, 3).astype(BF).reshape(strip, width, c1)
    shares = []
    for i, (row, rows) in enumerate(CHUNKS):
        shares.append(message(3 + i, q_send.at[row : row + rows], q_recv.at[row : row + rows], later))
        shares[i].start()
    for a in (2, 1):
        for b in range(3):
            weights_one[a, b].wait()
    acc_one[...] = conv_one_dot(2, 0, strip, 0, 2)
    def pick_last(rows):
        row = rows[halves - 1]
        for place in range(halves, strip):
            row = lax.select(last_row == place, rows[place], row)
        return row

    received[0].wait_recv()
    received[1].wait_recv()
    xsend[1] = pick_last(x_late)
    late_rims = [message(8, x_late.at[0], xlow.at[1], upper), message(9, xsend.at[1], xup.at[1], lower)]
    for copy in late_rims:
        copy.start()
    acc_one[:, c1 : 2 * c1] += conv_one_dot(3, 0, strip, 0, 1)
    load_up.wait()
    w_up[...] = jnp.zeros_like(w_up)
    w_up[:, 0:c2] = w_up_in[:, 0:c2]
    w_up[:, 256 : 256 + c2] = w_up_in[:, c2 : 2 * c2]
    received[2].wait_recv()
    pack_inner(1, 1, halves + 1, has_past)
    for copy in late_rims:
        copy.wait_recv()
    pack_one(1, 0, 1, has_past)
    pack_one(1, halves + 1, strip + 2, has_past)
    acc_one[...] += conv_one_dot(1, 0, strip, 1, 3)

    for copy in weights_two:
        copy.wait()
    w_two[:, :, 3 * c2 :] = jnp.zeros((3, 3, 64, c2), BF)

    def live(slot, row):
        return ((slot < frame_count) & (row < row_count)).astype(F32)

    def middle_rows(row, rows):
        cells = pl.ds(row * width, rows * width)
        for f in range(2):
            wide = x_own[f, row : row + rows].reshape(rows * width, c1).astype(F32)
            wide = wide + acc_one[cells, f * c1 : (f + 1) * c1]
            if f == 0:
                wide = wide + q_recv[row : row + rows].reshape(rows * width, c1).astype(F32) * has_past
            mid = wide.astype(BF)
            pair = jnp.dot(mid, w_up[...], preferred_element_type=F32)
            for s in range(2):
                half = pair[:, 256 * s : 256 * s + c2].astype(BF)
                ubuf[2 * f + s, row : row + rows] = half.reshape(rows, width, c2)

        def step(k, _):
            slot, place = k // rows, row + k % rows
            wide = ubuf[slot, place].astype(F32) * live(slot, place)
            ubuf[slot, place] = wide.astype(BF)
            ybuf[slot, place] = rms_silu(wide, gain_2, 1.0).astype(BF)
            return 0

        lax.fori_loop(0, 4 * rows, step, 0, unroll=4 * rows if rows < 4 else 8)

    def send_last(k, row, rows):
        def step(place, _):
            m1_send[place] = ybuf[jnp.maximum(frame_count - 1, 0), place]
            return 0

        lax.fori_loop(row, row + rows, step, 0, unroll=True)
        copy = message(k, m1_send.at[row : row + rows], tail_last.at[row : row + rows], later)
        copy.start()
        return copy

    def send_second(k, row, rows):
        def step(place, _):
            second = ybuf[jnp.maximum(frame_count - 2, 0), place]
            passed = (tail_last[place].astype(F32) * has_past).astype(BF)
            m2_send[place] = lax.select(frame_count >= 2, second, passed)
            return 0

        lax.fori_loop(row, row + rows, step, 0, unroll=True)
        copy = message(k, m2_send.at[row : row + rows], tail_second.at[row : row + rows], later)
        copy.start()
        return copy

    last = []
    for i, (row, rows) in enumerate(CHUNKS):
        shares[i].wait_recv()
        middle_rows(row, rows)
        last.append(send_last(12 + i, row, rows))

    for f in range(4):
        ysend[f] = ybuf[f, last_row]
    two_first = message(10, ybuf.at[:, 0], ylow, upper)
    two_last = message(11, ysend.at[0:4], yup, lower)
    two_first.start()
    two_last.start()

    def taps_two(f, s, raw, scale):
        left, middle, right = column_taps(raw.astype(F32) * scale)
        blank = jnp.zeros((width, 640 - 3 * c2), F32)
        act_two[f, s] = jnp.concatenate([left, middle, right, blank], axis=1).astype(BF)

    def pack_two(f, first, last, past, rows_of):
        def step(s, _):
            is_upper, is_lower = s == 0, (s == strip + 1) | (s - 1 == row_count)
            mine = rows_of(jnp.clip(s - 1, 0, strip - 1))
            raw = lax.select(is_upper, up_of[f][...], lax.select(is_lower, low_of[f][...], mine))
            scale = past * jnp.where(is_upper, has_upper, jnp.where(is_lower, has_lower, 1.0))
            taps_two(f, s, raw, scale)
            return 0

        lax.fori_loop(first, last, step, 0, unroll=True)

    def pack_two_inner(f, first, last, past, rows_of):
        def step(s, _):
            taps_two(f, s, rows_of(s - 1), past)
            return 0

        lax.fori_loop(first, last, step, 0, unroll=True)

    def rows_of(f):
        return lambda place: ybuf[f, place]

    def conv_two_dot(slots, taps, ranges):
        blocks = []
        for q in slots:
            for row, rows in ranges:
                planes = [
                    act_two[q + a, row + b : row + b + rows].reshape(rows * width, 640)
                    for a in taps
                    for b in range(3)
                ]
                blocks.append(jnp.concatenate(planes, axis=1))
        weight = w_two[taps[0] : taps[-1] + 1].reshape(len(taps) * 3 * 640, c2)
        total = jnp.dot(jnp.concatenate(blocks, axis=0), weight, preferred_element_type=F32)
        at, shares = 0, []
        for q in slots:
            for row, rows in ranges:
                shares.append((q, slice(row * width, (row + rows) * width), total[at : at + rows * width]))
                at += rows * width
        return shares

    def conv_two(slots, taps, ranges=((0, strip),)):
        for q, cells, share in conv_two_dot(slots, taps, ranges):
            acc_two[q, cells] = share

    def conv_two_more(slots, taps):
        for q, cells, share in conv_two_dot(slots, taps, ((0, strip),)):
            acc_two[q, cells] += share

    def finish(q):
        def step(place, _):
            wide = ubuf[q, place].astype(F32)
            conv = acc_two[q, pl.ds(pl.multiple_of(place * width, width), width)]
            out[q, place] = ((wide + conv) * live(q, place)).astype(BF)
            return 0

        lax.fori_loop(0, strip, step, 0, unroll=True)

    def pack_tail(f):
        of = lambda place: tail_of[f][place]
        pack_two(f, 0, 1, has_past, of)
        pack_two_inner(f, 1, halves + 1, has_past, of)
        pack_two(f, halves + 1, strip + 2, has_past, of)

    second = []
    for f in range(4):
        pack_two_inner(2 + f, 1, halves + 1, 1.0, rows_of(f))
    for i, (row, rows) in enumerate(CHUNKS[:-1]):
        last[i].wait_recv()
        second.append(send_second(15 + i, row, rows))
    two_first.wait_recv()
    two_last.wait_recv()
    for f in range(4):
        pack_two(2 + f, 0, 1, 1.0, rows_of(f))
        pack_two(2 + f, halves + 1, strip + 2, 1.0, rows_of(f))
    last[-1].wait_recv()
    second.append(send_second(15 + len(CHUNKS) - 1, *CHUNKS[-1]))
    ysend[4] = pick_last(tail_last)
    rims_last = [message(18, tail_last.at[0], low_last, upper), message(19, ysend.at[4], up_last, lower)]
    for copy in rims_last:
        copy.start()
    conv_two((3,), (0, 1, 2))
    conv_two((2,), (0, 1, 2))
    finish(3)
    finish(2)
    for copy in rims_last:
        copy.wait_recv()
    own_second = jnp.maximum(frame_count - 2, 0)
    for i, (of, passed) in enumerate(((yup, up_last), (ylow, low_last))):
        passed = (passed[...].astype(F32) * has_past).astype(BF)
        rim_send[i] = lax.select(frame_count >= 2, of[own_second], passed)
    rims_second = [message(20, rim_send.at[0], up_second, later), message(21, rim_send.at[1], low_second, later)]
    for copy in rims_second:
        copy.start()
    pack_tail(1)
    conv_two((1,), (0, 1, 2))
    finish(1)
    conv_two((0,), (1, 2))
    for copy in (*second, *rims_second):
        copy.wait_recv()
    pack_tail(0)
    conv_two_more((0,), (0,))
    finish(0)

    sent = [*received, rim_first, rim_last, *shares, *late_rims, *last]
    sent += [two_first, two_last, *second, *rims_last, *rims_second]
    for copy in sent:
        copy.wait_send()


def on_device(n_tm, n_rows, latents, gain_one, conv_one, up_weight, gain_two, conv_two, frame_counts, row_counts):
    frames, strip, width, c1 = latents.shape
    c2 = gain_two.shape[0]
    slots = 2 * frames
    cells = strip * width
    vmem = pltpu.VMEM
    scratch = [
        vmem((strip, width, c1), BF),
        vmem((strip, width, c1), BF),
        vmem((strip, width, c1), BF),
        vmem((2, strip, width, c1), BF),
        vmem((4, width, c1), BF),
        vmem((4, width, c1), BF),
        vmem((4, width, c1), BF),
        vmem((4, strip + 2, width, 3 * c1), BF),
        vmem((3, 3, c1, 3 * c1), BF),
        vmem((cells, 2 * c1), F32),
        vmem((c1, 2 * c2), BF),
        vmem((c1, 512), BF),
        vmem((slots, strip, width, c2), BF),
        vmem((slots, strip, width, c2), BF),
        vmem((4, width, c2), BF),
        vmem((4, width, c2), BF),
        vmem((width, c2), BF),
        vmem((width, c2), BF),
        vmem((width, c2), BF),
        vmem((width, c2), BF),
        vmem((2, width, c2), BF),
        vmem((5, width, c2), BF),
        vmem((strip, width, c2), BF),
        vmem((strip, width, c2), BF),
        vmem((strip, width, c2), BF),
        vmem((strip, width, c2), BF),
        vmem((6, strip + 2, width, 640), BF),
        vmem((3, 3, 3 * c2 + 64, c2), BF),
        vmem((slots, cells, c2), F32),
        pltpu.SemaphoreType.DMA((N_MSG,)),
        pltpu.SemaphoreType.DMA((N_MSG,)),
        pltpu.SemaphoreType.DMA((20,)),
    ]
    smem, anywhere = pl.BlockSpec(memory_space=pltpu.SMEM), pl.BlockSpec(memory_space=pl.ANY)
    in_vmem = pl.BlockSpec(memory_space=pltpu.VMEM)
    return pl.pallas_call(
        functools.partial(kernel, n_tm, n_rows),
        out_shape=pltpu.VMEM((slots, strip, width, c2), BF),
        in_specs=[smem, smem, anywhere, in_vmem, anywhere, anywhere, in_vmem, anywhere],
        out_specs=in_vmem,
        scratch_shapes=scratch,
        compiler_params=pltpu.CompilerParams(
            collective_id=0, has_side_effects=True, vmem_limit_bytes=60 * 2**20
        ),
    )(frame_counts, row_counts, latents, gain_one, conv_one, up_weight, gain_two, conv_two.reshape(3, 3, 3 * c2, c2))


def solution(mesh):
    in_specs = (P("tm", "rows", None, None), P(), P(), P(), P(), P(), P(), P())
    return jax.shard_map(
        functools.partial(on_device, mesh.shape["tm"], mesh.shape["rows"]),
        mesh=mesh, in_specs=in_specs, out_specs=P("tm", "rows", None, None), check_vma=False,
    )
```

```python
import functools

import jax
import jax.numpy as jnp
from jax import lax
from jax.experimental import pallas as pl
from jax.experimental.pallas import tpu as pltpu
from jax.sharding import PartitionSpec as P

MESH = pl.DeviceIdType.MESH
EPS = 1e-06
BF = jnp.bfloat16
F32 = jnp.float32
N_MSG = 22
CHUNKS = ((4, 4), (0, 4))


def rms_silu(wide, gain, scale):
    n = wide.shape[-1]
    mean = jnp.sum(wide * wide, axis=-1, keepdims=True) * (1.0 / n)
    half = wide * (lax.rsqrt(mean + EPS) * (0.5 * scale)) * gain
    return half * (1.0 + jnp.tanh(half))


def column_taps(act):
    width = act.shape[0]
    column = lax.broadcasted_iota(jnp.int32, act.shape, 0)
    left = jnp.where(column == 0, 0.0, pltpu.roll(act, 1, 0))
    right = jnp.where(column == width - 1, 0.0, pltpu.roll(act, width - 1, 0))
    return left, act, right


def kernel(
    n_tm, n_rows,
    frame_counts, row_counts, latents, gain_one, conv_one, up_weight, gain_two, conv_two,
    out,
    q_send, q_recv, x_late, x_own, xlow, xup, xsend, act_one, w_one, acc_one, w_up_in, w_up,
    ubuf, ybuf, ylow, yup, low_last, up_last, low_second, up_second, rim_send, ysend, m1_send, m2_send, tail_second, tail_last, act_two, w_two, acc_two,
    send_sem, recv_sem, load_sem,
):
    t, r = lax.axis_index("tm"), lax.axis_index("rows")
    later, earlier = (lax.rem(t + 1, n_tm), r), (lax.rem(t + n_tm - 1, n_tm), r)
    lower, upper = (t, lax.rem(r + 1, n_rows)), (t, lax.rem(r + n_rows - 1, n_rows))
    row_count, frame_count = row_counts[r], frame_counts[t]
    last_row = jnp.maximum(row_count - 1, 0)
    strip, width, c1 = x_late.shape
    x_of = (None, x_late, x_own.at[0], x_own.at[1])
    tail_of = (tail_second, tail_last)
    up_of = (up_second, up_last, *(yup.at[f] for f in range(4)))
    low_of = (low_second, low_last, *(ylow.at[f] for f in range(4)))
    c2 = ybuf.shape[-1]
    has_past = (t > 0).astype(F32)
    has_upper = (r > 0).astype(F32)
    has_lower = (r < n_rows - 1).astype(F32)

    def load(k, src, dst):
        return pltpu.make_async_copy(src, dst, load_sem.at[k])

    def message(k, src, dst, to):
        return pltpu.make_async_remote_copy(
            src_ref=src, dst_ref=dst, send_sem=send_sem.at[k], recv_sem=recv_sem.at[k],
            device_id=to, device_id_type=MESH,
        )

    own = load(0, latents, x_own)
    own.start()
    weights_one = {}
    for a in (2, 1, 0):
        for b in range(3):
            k = 1 + 3 * a + b
            weights_one[a, b] = load(
                k, conv_one.at[a, b], w_one.at[b, :, :, pl.ds((2 - a) * c1, c1)]
            )
    load_up = load(10, up_weight, w_up_in)
    weights_two = [
        load(11 + 3 * a + b, conv_two.at[a, b], w_two.at[a, b, pl.ds(0, 3 * c2)]) for a in range(3) for b in range(3)
    ]

    barrier = pltpu.get_barrier_semaphore()
    for place in (later, earlier, lower, upper):
        pl.semaphore_signal(barrier, inc=1, device_id=place, device_id_type=MESH)
    for a in (0, 2, 1):
        for b in range(3):
            weights_one[a, b].start()
    load_up.start()
    for copy in weights_two:
        copy.start()
    pl.semaphore_wait(barrier, 4)

    halves = strip // 2
    received = [
        message(i, latents.at[1, first:last], x_late.at[first:last], later)
        for i, (first, last) in enumerate(((0, 1), (halves - 1, strip), (1, halves - 1)))
    ]
    rim_first = message(6, latents.at[:, 0], xlow.at[2:4], upper)
    rim_last = message(7, xsend.at[2:4], xup.at[2:4], lower)
    rim_first.start()
    for copy in received:
        copy.start()
    own.wait()
    for f in (2, 3):
        xsend[f] = x_of[f][last_row]
    rim_last.start()

    gain_1 = gain_one[...].reshape(1, c1)
    gain_2 = gain_two[...].reshape(1, c2)

    def pack_one(f, first, last, past):
        def step(s, _):
            is_upper, is_lower = s == 0, (s == strip + 1) | (s - 1 == row_count)
            mine = x_of[f][jnp.clip(s - 1, 0, strip - 1)]
            raw = lax.select(is_upper, xup[f], lax.select(is_lower, xlow[f], mine))
            scale = past * jnp.where(is_upper, has_upper, jnp.where(is_lower, has_lower, 1.0))
            taps = column_taps(rms_silu(raw.astype(F32), gain_1, scale))
            for e in range(3):
                act_one[f, s, :, e * c1 : (e + 1) * c1] = taps[e].astype(BF)
            return 0

        lax.fori_loop(first, last, step, 0, unroll=True)

    def pack_inner(f, first, last, past):
        def step(s, _):
            taps = column_taps(rms_silu(x_of[f][s - 1].astype(F32), gain_1, past))
            for e in range(3):
                act_one[f, s, :, e * c1 : (e + 1) * c1] = taps[e].astype(BF)
            return 0

        lax.fori_loop(first, last, step, 0, unroll=True)

    def conv_one_dot(f, row, rows, first, last):
        planes = [act_one[f, row + b : row + b + rows].reshape(rows * width, 3 * c1) for b in range(3)]
        weight = w_one[:, :, :, first * c1 : last * c1].reshape(9 * c1, (last - first) * c1)
        return jnp.dot(jnp.concatenate(planes, axis=1), weight, preferred_element_type=F32)

    for f in (2, 3):
        pack_inner(f, 1, 5, 1.0)
    rim_first.wait_recv()
    rim_last.wait_recv()
    for f in (2, 3):
        pack_one(f, 0, 1, 1.0)
        pack_one(f, 5, 10, 1.0)

    for b in range(3):
        weights_one[0, b].wait()
    q_send[...] = conv_one_dot(2, 0, strip, 2, 3).astype(BF).reshape(strip, width, c1)
    shares = []
    for i, (row, rows) in enumerate(CHUNKS):
        shares.append(message(3 + i, q_send.at[row : row + rows], q_recv.at[row : row + rows], later))
        shares[i].start()
    for a in (2, 1):
        for b in range(3):
            weights_one[a, b].wait()
    acc_one[...] = conv_one_dot(2, 0, strip, 0, 2)
    def pick_last(rows):
        row = rows[halves - 1]
        for place in range(halves, strip):
            row = lax.select(last_row == place, rows[place], row)
        return row

    received[0].wait_recv()
    received[1].wait_recv()
    xsend[1] = pick_last(x_late)
    late_rims = [message(8, x_late.at[0], xlow.at[1], upper), message(9, xsend.at[1], xup.at[1], lower)]
    for copy in late_rims:
        copy.start()
    acc_one[:, c1 : 2 * c1] += conv_one_dot(3, 0, strip, 0, 1)
    load_up.wait()
    w_up[...] = jnp.zeros_like(w_up)
    w_up[:, 0:c2] = w_up_in[:, 0:c2]
    w_up[:, 256 : 256 + c2] = w_up_in[:, c2 : 2 * c2]
    received[2].wait_recv()
    pack_inner(1, 1, halves + 1, has_past)
    for copy in late_rims:
        copy.wait_recv()
    pack_one(1, 0, 1, has_past)
    pack_one(1, halves + 1, strip + 2, has_past)
    acc_one[...] += conv_one_dot(1, 0, strip, 1, 3)

    for copy in weights_two:
        copy.wait()
    w_two[:, :, 3 * c2 :] = jnp.zeros((3, 3, 64, c2), BF)

    def live(slot, row):
        return ((slot < frame_count) & (row < row_count)).astype(F32)

    def middle_rows(row, rows):
        cells = pl.ds(row * width, rows * width)
        for f in range(2):
            wide = x_own[f, row : row + rows].reshape(rows * width, c1).astype(F32)
            wide = wide + acc_one[cells, f * c1 : (f + 1) * c1]
            if f == 0:
                wide = wide + q_recv[row : row + rows].reshape(rows * width, c1).astype(F32) * has_past
            mid = wide.astype(BF)
            pair = jnp.dot(mid, w_up[...], preferred_element_type=F32)
            for s in range(2):
                for place in range(row, row + rows):
                    at = (place - row) * width
                    half = pair[at : at + width, 256 * s : 256 * s + c2].astype(BF)
                    wide = half.astype(F32) * live(2 * f + s, place)
                    ubuf[2 * f + s, place] = wide.astype(BF)
                    ybuf[2 * f + s, place] = rms_silu(wide, gain_2, 1.0).astype(BF)

    def send_last(k, row, rows):
        def step(place, _):
            m1_send[place] = ybuf[jnp.maximum(frame_count - 1, 0), place]
            return 0

        lax.fori_loop(row, row + rows, step, 0, unroll=True)
        copy = message(k, m1_send.at[row : row + rows], tail_last.at[row : row + rows], later)
        copy.start()
        return copy

    def send_second(k, row, rows):
        def step(place, _):
            second = ybuf[jnp.maximum(frame_count - 2, 0), place]
            passed = (tail_last[place].astype(F32) * has_past).astype(BF)
            m2_send[place] = lax.select(frame_count >= 2, second, passed)
            return 0

        lax.fori_loop(row, row + rows, step, 0, unroll=True)
        copy = message(k, m2_send.at[row : row + rows], tail_second.at[row : row + rows], later)
        copy.start()
        return copy

    last = []
    for i, (row, rows) in enumerate(CHUNKS):
        shares[i].wait_recv()
        middle_rows(row, rows)
        last.append(send_last(12 + i, row, rows))

    for f in range(4):
        ysend[f] = ybuf[f, last_row]
    two_first = message(10, ybuf.at[:, 0], ylow, upper)
    two_last = message(11, ysend.at[0:4], yup, lower)
    two_first.start()
    two_last.start()

    def taps_two(f, s, raw, scale):
        left, middle, right = column_taps(raw.astype(F32) * scale)
        blank = jnp.zeros((width, 640 - 3 * c2), F32)
        act_two[f, s] = jnp.concatenate([left, middle, right, blank], axis=1).astype(BF)

    def pack_two(f, first, last, past, rows_of):
        def step(s, _):
            is_upper, is_lower = s == 0, (s == strip + 1) | (s - 1 == row_count)
            mine = rows_of(jnp.clip(s - 1, 0, strip - 1))
            raw = lax.select(is_upper, up_of[f][...], lax.select(is_lower, low_of[f][...], mine))
            scale = past * jnp.where(is_upper, has_upper, jnp.where(is_lower, has_lower, 1.0))
            taps_two(f, s, raw, scale)
            return 0

        lax.fori_loop(first, last, step, 0, unroll=True)

    def pack_two_inner(f, first, last, past, rows_of):
        def step(s, _):
            taps_two(f, s, rows_of(s - 1), past)
            return 0

        lax.fori_loop(first, last, step, 0, unroll=True)

    def rows_of(f):
        return lambda place: ybuf[f, place]

    def conv_two_dot(slots, taps, ranges):
        blocks = []
        for q in slots:
            for row, rows in ranges:
                planes = [
                    act_two[q + a, row + b : row + b + rows].reshape(rows * width, 640)
                    for a in taps
                    for b in range(3)
                ]
                blocks.append(jnp.concatenate(planes, axis=1))
        weight = w_two[taps[0] : taps[-1] + 1].reshape(len(taps) * 3 * 640, c2)
        total = jnp.dot(jnp.concatenate(blocks, axis=0), weight, preferred_element_type=F32)
        at, shares = 0, []
        for q in slots:
            for row, rows in ranges:
                shares.append((q, slice(row * width, (row + rows) * width), total[at : at + rows * width]))
                at += rows * width
        return shares

    def conv_two(slots, taps, ranges=((0, strip),)):
        for q, cells, share in conv_two_dot(slots, taps, ranges):
            acc_two[q, cells] = share

    def conv_two_more(slots, taps):
        for q, cells, share in conv_two_dot(slots, taps, ((0, strip),)):
            acc_two[q, cells] += share

    def finish(q):
        def step(place, _):
            wide = ubuf[q, place].astype(F32)
            conv = acc_two[q, pl.ds(pl.multiple_of(place * width, width), width)]
            out[q, place] = ((wide + conv) * live(q, place)).astype(BF)
            return 0

        lax.fori_loop(0, strip, step, 0, unroll=True)

    def pack_tail(f):
        of = lambda place: tail_of[f][place]
        pack_two(f, 0, 1, has_past, of)
        pack_two_inner(f, 1, halves + 1, has_past, of)
        pack_two(f, halves + 1, strip + 2, has_past, of)

    second = []
    for f in range(4):
        pack_two_inner(2 + f, 1, halves + 1, 1.0, rows_of(f))
    for i, (row, rows) in enumerate(CHUNKS[:-1]):
        last[i].wait_recv()
        second.append(send_second(15 + i, row, rows))
    two_first.wait_recv()
    two_last.wait_recv()
    for f in range(4):
        pack_two(2 + f, 0, 1, 1.0, rows_of(f))
        pack_two(2 + f, halves + 1, strip + 2, 1.0, rows_of(f))
    last[-1].wait_recv()
    second.append(send_second(15 + len(CHUNKS) - 1, *CHUNKS[-1]))
    ysend[4] = pick_last(tail_last)
    rims_last = [message(18, tail_last.at[0], low_last, upper), message(19, ysend.at[4], up_last, lower)]
    for copy in rims_last:
        copy.start()
    conv_two((3,), (0, 1, 2))
    conv_two((2,), (0, 1, 2))
    finish(3)
    finish(2)
    for copy in rims_last:
        copy.wait_recv()
    own_second = jnp.maximum(frame_count - 2, 0)
    for i, (of, passed) in enumerate(((yup, up_last), (ylow, low_last))):
        passed = (passed[...].astype(F32) * has_past).astype(BF)
        rim_send[i] = lax.select(frame_count >= 2, of[own_second], passed)
    rims_second = [message(20, rim_send.at[0], up_second, later), message(21, rim_send.at[1], low_second, later)]
    for copy in rims_second:
        copy.start()
    pack_tail(1)
    conv_two((1,), (0, 1, 2))
    finish(1)
    conv_two((0,), (1, 2))
    for copy in (*second, *rims_second):
        copy.wait_recv()
    pack_tail(0)
    conv_two_more((0,), (0,))
    finish(0)

    sent = [*received, rim_first, rim_last, *shares, *late_rims, *last]
    sent += [two_first, two_last, *second, *rims_last, *rims_second]
    for copy in sent:
        copy.wait_send()


def on_device(n_tm, n_rows, latents, gain_one, conv_one, up_weight, gain_two, conv_two, frame_counts, row_counts):
    frames, strip, width, c1 = latents.shape
    c2 = gain_two.shape[0]
    slots = 2 * frames
    cells = strip * width
    vmem = pltpu.VMEM
    scratch = [
        vmem((strip, width, c1), BF),
        vmem((strip, width, c1), BF),
        vmem((strip, width, c1), BF),
        vmem((2, strip, width, c1), BF),
        vmem((4, width, c1), BF),
        vmem((4, width, c1), BF),
        vmem((4, width, c1), BF),
        vmem((4, strip + 2, width, 3 * c1), BF),
        vmem((3, 3, c1, 3 * c1), BF),
        vmem((cells, 2 * c1), F32),
        vmem((c1, 2 * c2), BF),
        vmem((c1, 512), BF),
        vmem((slots, strip, width, c2), BF),
        vmem((slots, strip, width, c2), BF),
        vmem((4, width, c2), BF),
        vmem((4, width, c2), BF),
        vmem((width, c2), BF),
        vmem((width, c2), BF),
        vmem((width, c2), BF),
        vmem((width, c2), BF),
        vmem((2, width, c2), BF),
        vmem((5, width, c2), BF),
        vmem((strip, width, c2), BF),
        vmem((strip, width, c2), BF),
        vmem((strip, width, c2), BF),
        vmem((strip, width, c2), BF),
        vmem((6, strip + 2, width, 640), BF),
        vmem((3, 3, 3 * c2 + 64, c2), BF),
        vmem((slots, cells, c2), F32),
        pltpu.SemaphoreType.DMA((N_MSG,)),
        pltpu.SemaphoreType.DMA((N_MSG,)),
        pltpu.SemaphoreType.DMA((20,)),
    ]
    smem, anywhere = pl.BlockSpec(memory_space=pltpu.SMEM), pl.BlockSpec(memory_space=pl.ANY)
    in_vmem = pl.BlockSpec(memory_space=pltpu.VMEM)
    return pl.pallas_call(
        functools.partial(kernel, n_tm, n_rows),
        out_shape=pltpu.VMEM((slots, strip, width, c2), BF),
        in_specs=[smem, smem, anywhere, in_vmem, anywhere, anywhere, in_vmem, anywhere],
        out_specs=in_vmem,
        scratch_shapes=scratch,
        compiler_params=pltpu.CompilerParams(
            collective_id=0, has_side_effects=True, vmem_limit_bytes=60 * 2**20
        ),
    )(frame_counts, row_counts, latents, gain_one, conv_one, up_weight, gain_two, conv_two.reshape(3, 3, 3 * c2, c2))


def solution(mesh):
    in_specs = (P("tm", "rows", None, None), P(), P(), P(), P(), P(), P(), P())
    return jax.shard_map(
        functools.partial(on_device, mesh.shape["tm"], mesh.shape["rows"]),
        mesh=mesh, in_specs=in_specs, out_specs=P("tm", "rows", None, None), check_vma=False,
    )
```

```python
import functools

import jax
import jax.numpy as jnp
from jax import lax
from jax.experimental import pallas as pl
from jax.experimental.pallas import tpu as pltpu
from jax.sharding import PartitionSpec as P

MESH = pl.DeviceIdType.MESH
EPS = 1e-06
BF = jnp.bfloat16
F32 = jnp.float32
N_MSG = 22
CHUNKS = ((4, 4), (0, 4))


def rms_silu(wide, gain, scale):
    n = wide.shape[-1]
    mean = jnp.sum(wide * wide, axis=-1, keepdims=True) * (1.0 / n)
    half = wide * (lax.rsqrt(mean + EPS) * (0.5 * scale)) * gain
    return half * (1.0 + jnp.tanh(half))


def column_taps(act):
    width = act.shape[0]
    column = lax.broadcasted_iota(jnp.int32, act.shape, 0)
    left = jnp.where(column == 0, 0.0, pltpu.roll(act, 1, 0))
    right = jnp.where(column == width - 1, 0.0, pltpu.roll(act, width - 1, 0))
    return left, act, right


def kernel(
    n_tm, n_rows,
    frame_counts, row_counts, latents, gain_one, conv_one, up_weight, gain_two, conv_two,
    out,
    q_send, q_recv, x_late, x_own, xlow, xup, xsend, act_one, w_one, acc_one, w_up_in, w_up,
    ubuf, ybuf, ylow, yup, low_last, up_last, low_second, up_second, rim_send, ysend, m1_send, m2_send, tail_second, tail_last, act_two, w_two, acc_two,
    send_sem, recv_sem, load_sem,
):
    t, r = lax.axis_index("tm"), lax.axis_index("rows")
    later, earlier = (lax.rem(t + 1, n_tm), r), (lax.rem(t + n_tm - 1, n_tm), r)
    lower, upper = (t, lax.rem(r + 1, n_rows)), (t, lax.rem(r + n_rows - 1, n_rows))
    row_count, frame_count = row_counts[r], frame_counts[t]
    last_row = jnp.maximum(row_count - 1, 0)
    strip, width, c1 = x_late.shape
    x_of = (None, x_late, x_own.at[0], x_own.at[1])
    tail_of = (tail_second, tail_last)
    up_of = (up_second, up_last, *(yup.at[f] for f in range(4)))
    low_of = (low_second, low_last, *(ylow.at[f] for f in range(4)))
    c2 = ybuf.shape[-1]
    has_past = (t > 0).astype(F32)
    has_upper = (r > 0).astype(F32)
    has_lower = (r < n_rows - 1).astype(F32)

    def load(k, src, dst):
        return pltpu.make_async_copy(src, dst, load_sem.at[k])

    def message(k, src, dst, to):
        return pltpu.make_async_remote_copy(
            src_ref=src, dst_ref=dst, send_sem=send_sem.at[k], recv_sem=recv_sem.at[k],
            device_id=to, device_id_type=MESH,
        )

    own = load(0, latents, x_own)
    own.start()
    weights_one = {}
    for a in (2, 1, 0):
        for b in range(3):
            k = 1 + 3 * a + b
            weights_one[a, b] = load(
                k, conv_one.at[a, b], w_one.at[b, :, :, pl.ds((2 - a) * c1, c1)]
            )
    load_up = load(10, up_weight, w_up_in)
    weights_two = [
        load(11 + 3 * a + b, conv_two.at[a, b], w_two.at[a, b, pl.ds(0, 3 * c2)]) for a in range(3) for b in range(3)
    ]

    barrier = pltpu.get_barrier_semaphore()
    for place in (later, earlier, lower, upper):
        pl.semaphore_signal(barrier, inc=1, device_id=place, device_id_type=MESH)
    for a in (0, 2, 1):
        for b in range(3):
            weights_one[a, b].start()
    load_up.start()
    for copy in weights_two:
        copy.start()
    pl.semaphore_wait(barrier, 4)

    halves = strip // 2
    received = [
        message(i, latents.at[1, first:last], x_late.at[first:last], later)
        for i, (first, last) in enumerate(((0, 1), (halves - 1, strip), (1, halves - 1)))
    ]
    rim_first = message(6, latents.at[:, 0], xlow.at[2:4], upper)
    rim_last = message(7, xsend.at[2:4], xup.at[2:4], lower)
    rim_first.start()
    for copy in received:
        copy.start()
    own.wait()
    for f in (2, 3):
        xsend[f] = x_of[f][last_row]
    rim_last.start()

    gain_1 = gain_one[...].reshape(1, c1)
    gain_2 = gain_two[...].reshape(1, c2)

    def pack_one(f, first, last, past):
        def step(s, _):
            is_upper, is_lower = s == 0, (s == strip + 1) | (s - 1 == row_count)
            mine = x_of[f][jnp.clip(s - 1, 0, strip - 1)]
            raw = lax.select(is_upper, xup[f], lax.select(is_lower, xlow[f], mine))
            scale = past * jnp.where(is_upper, has_upper, jnp.where(is_lower, has_lower, 1.0))
            taps = column_taps(rms_silu(raw.astype(F32), gain_1, scale))
            for e in range(3):
                act_one[f, s, :, e * c1 : (e + 1) * c1] = taps[e].astype(BF)
            return 0

        lax.fori_loop(first, last, step, 0, unroll=True)

    def pack_inner(f, first, last, past):
        def step(s, _):
            taps = column_taps(rms_silu(x_of[f][s - 1].astype(F32), gain_1, past))
            for e in range(3):
                act_one[f, s, :, e * c1 : (e + 1) * c1] = taps[e].astype(BF)
            return 0

        lax.fori_loop(first, last, step, 0, unroll=True)

    def conv_one_dot(f, row, rows, first, last):
        planes = [act_one[f, row + b : row + b + rows].reshape(rows * width, 3 * c1) for b in range(3)]
        weight = w_one[:, :, :, first * c1 : last * c1].reshape(9 * c1, (last - first) * c1)
        return jnp.dot(jnp.concatenate(planes, axis=1), weight, preferred_element_type=F32)

    for f in (2, 3):
        pack_inner(f, 1, 5, 1.0)
    rim_first.wait_recv()
    rim_last.wait_recv()
    for f in (2, 3):
        pack_one(f, 0, 1, 1.0)
        pack_one(f, 5, 10, 1.0)

    for b in range(3):
        weights_one[0, b].wait()
    q_send[...] = conv_one_dot(2, 0, strip, 2, 3).astype(BF).reshape(strip, width, c1)
    shares = []
    for i, (row, rows) in enumerate(CHUNKS):
        shares.append(message(3 + i, q_send.at[row : row + rows], q_recv.at[row : row + rows], later))
        shares[i].start()
    for a in (2, 1):
        for b in range(3):
            weights_one[a, b].wait()
    acc_one[...] = conv_one_dot(2, 0, strip, 0, 2)
    def pick_last(rows):
        row = rows[halves - 1]
        for place in range(halves, strip):
            row = lax.select(last_row == place, rows[place], row)
        return row

    received[0].wait_recv()
    received[1].wait_recv()
    xsend[1] = pick_last(x_late)
    late_rims = [message(8, x_late.at[0], xlow.at[1], upper), message(9, xsend.at[1], xup.at[1], lower)]
    for copy in late_rims:
        copy.start()
    acc_one[:, c1 : 2 * c1] += conv_one_dot(3, 0, strip, 0, 1)
    load_up.wait()
    w_up[...] = jnp.zeros_like(w_up)
    w_up[:, 0:c2] = w_up_in[:, 0:c2]
    w_up[:, 256 : 256 + c2] = w_up_in[:, c2 : 2 * c2]
    received[2].wait_recv()
    pack_inner(1, 1, halves + 1, has_past)
    for copy in late_rims:
        copy.wait_recv()
    pack_one(1, 0, 1, has_past)
    pack_one(1, halves + 1, strip + 2, has_past)
    acc_one[...] += conv_one_dot(1, 0, strip, 1, 3)

    for copy in weights_two:
        copy.wait()
    w_two[:, :, 3 * c2 :] = jnp.zeros((3, 3, 64, c2), BF)

    def live(slot, row):
        return ((slot < frame_count) & (row < row_count)).astype(F32)

    def middle_rows(row, rows):
        cells = pl.ds(row * width, rows * width)
        for f in range(2):
            wide = x_own[f, row : row + rows].reshape(rows * width, c1).astype(F32)
            wide = wide + acc_one[cells, f * c1 : (f + 1) * c1]
            if f == 0:
                wide = wide + q_recv[row : row + rows].reshape(rows * width, c1).astype(F32) * has_past
            mid = wide.astype(BF)
            pair = jnp.dot(mid, w_up[...], preferred_element_type=F32)
            for s in range(2):
                for place in range(row, row + rows):
                    at = (place - row) * width
                    half = pair[at : at + width, 256 * s : 256 * s + c2].astype(BF)
                    wide = half.astype(F32) * live(2 * f + s, place)
                    ubuf[2 * f + s, place] = wide.astype(BF)
                    ybuf[2 * f + s, place] = rms_silu(wide, gain_2, 1.0).astype(BF)

    def send_last(k, row, rows):
        def step(place, _):
            m1_send[place] = ybuf[jnp.maximum(frame_count - 1, 0), place]
            return 0

        lax.fori_loop(row, row + rows, step, 0, unroll=True)
        copy = message(k, m1_send.at[row : row + rows], tail_last.at[row : row + rows], later)
        copy.start()
        return copy

    def send_second(k, row, rows):
        def step(place, _):
            second = ybuf[jnp.maximum(frame_count - 2, 0), place]
            passed = (tail_last[place].astype(F32) * has_past).astype(BF)
            m2_send[place] = lax.select(frame_count >= 2, second, passed)
            return 0

        lax.fori_loop(row, row + rows, step, 0, unroll=True)
        copy = message(k, m2_send.at[row : row + rows], tail_second.at[row : row + rows], later)
        copy.start()
        return copy

    last = []
    for i, (row, rows) in enumerate(CHUNKS):
        shares[i].wait_recv()
        middle_rows(row, rows)
        last.append(send_last(12 + i, row, rows))

    for f in range(4):
        ysend[f] = ybuf[f, last_row]
    two_first = message(10, ybuf.at[:, 0], ylow, upper)
    two_last = message(11, ysend.at[0:4], yup, lower)
    two_first.start()
    two_last.start()

    def taps_two(f, s, raw, scale):
        left, middle, right = column_taps(raw.astype(F32) * scale)
        blank = jnp.zeros((width, 640 - 3 * c2), F32)
        act_two[f, s] = jnp.concatenate([left, middle, right, blank], axis=1).astype(BF)

    def pack_two(f, first, last, past, rows_of):
        def step(s, _):
            is_upper, is_lower = s == 0, (s == strip + 1) | (s - 1 == row_count)
            mine = rows_of(jnp.clip(s - 1, 0, strip - 1))
            raw = lax.select(is_upper, up_of[f][...], lax.select(is_lower, low_of[f][...], mine))
            scale = past * jnp.where(is_upper, has_upper, jnp.where(is_lower, has_lower, 1.0))
            taps_two(f, s, raw, scale)
            return 0

        lax.fori_loop(first, last, step, 0, unroll=True)

    def pack_two_inner(f, first, last, past, rows_of):
        def step(s, _):
            taps_two(f, s, rows_of(s - 1), past)
            return 0

        lax.fori_loop(first, last, step, 0, unroll=True)

    def rows_of(f):
        return lambda place: ybuf[f, place]

    def conv_two_dot(slots, taps, ranges):
        blocks = []
        for q in slots:
            for row, rows in ranges:
                planes = [
                    act_two[q + a, row + b : row + b + rows].reshape(rows * width, 640)
                    for a in taps
                    for b in range(3)
                ]
                blocks.append(jnp.concatenate(planes, axis=1))
        weight = w_two[taps[0] : taps[-1] + 1].reshape(len(taps) * 3 * 640, c2)
        total = jnp.dot(jnp.concatenate(blocks, axis=0), weight, preferred_element_type=F32)
        at, shares = 0, []
        for q in slots:
            for row, rows in ranges:
                shares.append((q, slice(row * width, (row + rows) * width), total[at : at + rows * width]))
                at += rows * width
        return shares

    def conv_two(slots, taps, ranges=((0, strip),)):
        for q, cells, share in conv_two_dot(slots, taps, ranges):
            acc_two[q, cells] = share

    def conv_two_more(slots, taps):
        for q, cells, share in conv_two_dot(slots, taps, ((0, strip),)):
            acc_two[q, cells] += share

    def finish(q):
        def step(place, _):
            wide = ubuf[q, place].astype(F32)
            conv = acc_two[q, pl.ds(pl.multiple_of(place * width, width), width)]
            out[q, place] = ((wide + conv) * live(q, place)).astype(BF)
            return 0

        lax.fori_loop(0, strip, step, 0, unroll=True)

    def pack_tail(f):
        of = lambda place: tail_of[f][place]
        pack_two(f, 0, 1, has_past, of)
        pack_two(f, halves + 1, strip + 2, has_past, of)

    second = []
    for f in range(4):
        pack_two_inner(2 + f, 1, halves + 1, 1.0, rows_of(f))
    for i, (row, rows) in enumerate(CHUNKS[:-1]):
        last[i].wait_recv()
        second.append(send_second(15 + i, row, rows))
    two_first.wait_recv()
    two_last.wait_recv()
    for f in range(4):
        pack_two(2 + f, 0, 1, 1.0, rows_of(f))
        pack_two(2 + f, halves + 1, strip + 2, 1.0, rows_of(f))
    last[-1].wait_recv()
    second.append(send_second(15 + len(CHUNKS) - 1, *CHUNKS[-1]))
    ysend[4] = pick_last(tail_last)
    rims_last = [message(18, tail_last.at[0], low_last, upper), message(19, ysend.at[4], up_last, lower)]
    for copy in rims_last:
        copy.start()
    conv_two((3,), (0, 1, 2))
    conv_two((2,), (0, 1, 2))
    finish(3)
    finish(2)
    pack_two_inner(1, 1, halves + 1, has_past, lambda place: tail_last[place])
    for copy in rims_last:
        copy.wait_recv()
    own_second = jnp.maximum(frame_count - 2, 0)
    for i, (of, passed) in enumerate(((yup, up_last), (ylow, low_last))):
        passed = (passed[...].astype(F32) * has_past).astype(BF)
        rim_send[i] = lax.select(frame_count >= 2, of[own_second], passed)
    rims_second = [message(20, rim_send.at[0], up_second, later), message(21, rim_send.at[1], low_second, later)]
    for copy in rims_second:
        copy.start()
    pack_tail(1)
    conv_two((1,), (0, 1, 2))
    finish(1)
    conv_two((0,), (1, 2))
    for copy in second:
        copy.wait_recv()
    pack_two_inner(0, 1, halves + 1, has_past, lambda place: tail_second[place])
    for copy in rims_second:
        copy.wait_recv()
    pack_tail(0)
    conv_two_more((0,), (0,))
    finish(0)

    sent = [*received, rim_first, rim_last, *shares, *late_rims, *last]
    sent += [two_first, two_last, *second, *rims_last, *rims_second]
    for copy in sent:
        copy.wait_send()


def on_device(n_tm, n_rows, latents, gain_one, conv_one, up_weight, gain_two, conv_two, frame_counts, row_counts):
    frames, strip, width, c1 = latents.shape
    c2 = gain_two.shape[0]
    slots = 2 * frames
    cells = strip * width
    vmem = pltpu.VMEM
    scratch = [
        vmem((strip, width, c1), BF),
        vmem((strip, width, c1), BF),
        vmem((strip, width, c1), BF),
        vmem((2, strip, width, c1), BF),
        vmem((4, width, c1), BF),
        vmem((4, width, c1), BF),
        vmem((4, width, c1), BF),
        vmem((4, strip + 2, width, 3 * c1), BF),
        vmem((3, 3, c1, 3 * c1), BF),
        vmem((cells, 2 * c1), F32),
        vmem((c1, 2 * c2), BF),
        vmem((c1, 512), BF),
        vmem((slots, strip, width, c2), BF),
        vmem((slots, strip, width, c2), BF),
        vmem((4, width, c2), BF),
        vmem((4, width, c2), BF),
        vmem((width, c2), BF),
        vmem((width, c2), BF),
        vmem((width, c2), BF),
        vmem((width, c2), BF),
        vmem((2, width, c2), BF),
        vmem((5, width, c2), BF),
        vmem((strip, width, c2), BF),
        vmem((strip, width, c2), BF),
        vmem((strip, width, c2), BF),
        vmem((strip, width, c2), BF),
        vmem((6, strip + 2, width, 640), BF),
        vmem((3, 3, 3 * c2 + 64, c2), BF),
        vmem((slots, cells, c2), F32),
        pltpu.SemaphoreType.DMA((N_MSG,)),
        pltpu.SemaphoreType.DMA((N_MSG,)),
        pltpu.SemaphoreType.DMA((20,)),
    ]
    smem, anywhere = pl.BlockSpec(memory_space=pltpu.SMEM), pl.BlockSpec(memory_space=pl.ANY)
    in_vmem = pl.BlockSpec(memory_space=pltpu.VMEM)
    return pl.pallas_call(
        functools.partial(kernel, n_tm, n_rows),
        out_shape=pltpu.VMEM((slots, strip, width, c2), BF),
        in_specs=[smem, smem, anywhere, in_vmem, anywhere, anywhere, in_vmem, anywhere],
        out_specs=in_vmem,
        scratch_shapes=scratch,
        compiler_params=pltpu.CompilerParams(
            collective_id=0, has_side_effects=True, vmem_limit_bytes=60 * 2**20
        ),
    )(frame_counts, row_counts, latents, gain_one, conv_one, up_weight, gain_two, conv_two.reshape(3, 3, 3 * c2, c2))


def solution(mesh):
    in_specs = (P("tm", "rows", None, None), P(), P(), P(), P(), P(), P(), P())
    return jax.shard_map(
        functools.partial(on_device, mesh.shape["tm"], mesh.shape["rows"]),
        mesh=mesh, in_specs=in_specs, out_specs=P("tm", "rows", None, None), check_vma=False,
    )
```
